256 devices in a mesh: row: 4 (over y_lo, core), col: 16 (over y_hi, z), layer: 4 (over x).
Axes of the slice: x: 4, y: 4 (y_hi: 2, y_lo: 2; y = y_hi * 2 + y_lo), z: 8, core: 2. Of those that a mesh axis runs over, the one named last changes fastest.
Arguments:
- left_panels: bfloat16 [4, 16, 4, 16, 128, 128], P('row', 'col', 'layer'), may hold values from -6 to 6
- right_panels: bfloat16 [4, 16, 4, 64, 128, 128], P('row', 'col', 'layer'), may hold values from -0.5 to 0.5
- pair_lists: int32 [4, 16, 4, 3, 3, 256], P('row', 'col', 'layer'), may hold values from 0 to 63, as said below
Outputs:
- product_tiles: float32 [4, 16, 16, 128, 128], P('row', 'col', 'layer')
The draws below stay inside these ranges and needn't reach their ends.
Inputs may be any that keep to these rules, and one draw needn't show every extreme that they name: `pair_lists`: entry 0 of the second to last dimension is an A block below 16, entry 1 a B block below 64, entry 2 a C block below 16 or 16 for an empty slot. At each grid position, layer and step the used slots come first; at least one grid position, layer and step uses all 256 slots.
All inputs are finite; a program needn't handle non-finite values.
Results may differ from the reference program's by a relative error of at most 0.0003.
Values may be sent and summed in bfloat16 or wider, within the bound.
A program may use at most 64 MiB of HBM per device.

```python
import jax
import jax.numpy as jnp
from jax import lax

BS = 128
STEPS = 3
TA = 16
TB = 64
NC = 16
NP = 256
N_ROW = 4
N_COL = 16
N_LAYER = 4


def draw_pair_lists(key, part):
    key = jax.random.fold_in(key, 7)
    keys = jax.random.split(key, 5)
    grid_shape = (N_ROW, N_COL, N_LAYER, STEPS)
    counts = jax.random.randint(keys[0], grid_shape, NP // 8, NP // 2 + 1, dtype=jnp.int32)
    flat_counts = counts.reshape(-1)
    busiest = jax.random.randint(keys[1], (), 0, flat_counts.shape[0], dtype=jnp.int32)
    flat_counts = flat_counts.at[busiest].set(NP)
    counts = flat_counts.reshape(grid_shape)
    full_shape = grid_shape + (NP,)
    left_ids = jax.random.randint(keys[2], full_shape, 0, TA, dtype=jnp.int32)
    right_ids = jax.random.randint(keys[3], full_shape, 0, TB, dtype=jnp.int32)
    target_ids = jax.random.randint(keys[4], full_shape, 0, NC, dtype=jnp.int32)
    slot_ids = lax.broadcasted_iota(jnp.int32, full_shape, 4)
    target_ids = jnp.where(slot_ids < counts[..., None], target_ids, NC)
    return jnp.stack([left_ids, right_ids, target_ids], axis=4)


def block_levels(stream_key, dims, pieces, least, high):
    def one(dim, shards_of):
        heights = jax.random.uniform(jax.random.fold_in(jax.random.fold_in(stream_key, 6), dim), (shards_of,), jnp.float32, least / len(pieces), high / len(pieces))
        return jnp.repeat(jnp.exp(heights), dims[dim] // shards_of).reshape((-1,) + (1,) * (len(dims) - dim - 1))

    gain = one(*pieces[0])
    for cut in pieces[1:]:
        gain = gain * one(*cut)
    return gain


def gaussian(rng, extent, deviation, limit, cuts=(), held_as=jnp.bfloat16):
    entries = deviation * jax.random.normal(rng, extent, jnp.float32)
    if cuts:
        entries = entries * block_levels(rng, extent, cuts, -0.22, 0.18)
    return jnp.clip(entries, -limit, limit).astype(held_as)


def setup_inputs(seed: int = 0) -> dict:
    streams_of = jax.random.split(jax.random.key(seed), 4)
    return {
        "left_panels": gaussian(streams_of[0], (N_ROW, N_COL, N_LAYER, TA, BS, BS), 1.0, 6.0, ((0, 4), (1, 16), (2, 4))),
        "right_panels": gaussian(streams_of[1], (N_ROW, N_COL, N_LAYER, TB, BS, BS), BS ** -0.5, 0.5, ((0, 4), (1, 16), (2, 4))),
        "pair_lists": draw_pair_lists(jax.random.fold_in(streams_of[3], 71), 0),
    }


def reference(left_panels, right_panels, pair_lists):
    def position(flat_index):
        row_index = flat_index // N_COL
        col_index = flat_index % N_COL
        running = jnp.zeros((NC + 1, BS, BS), jnp.float32)
        for layer_index in range(N_LAYER):
            for turn_index in range(STEPS):
                left_stack = left_panels[jnp.mod(row_index - turn_index, N_ROW), col_index, layer_index]
                right_stack = right_panels[row_index, jnp.mod(col_index - turn_index, N_COL), layer_index]
                chosen = pair_lists[row_index, col_index, layer_index, turn_index]
                left_tiles = jnp.take(left_stack, chosen[0], axis=0).astype(jnp.float32)
                right_tiles = jnp.take(right_stack, chosen[1], axis=0).astype(jnp.float32)
                products = jnp.einsum("pij,pjk->pik", left_tiles, right_tiles, precision=lax.Precision.HIGHEST)
                running = running + jax.ops.segment_sum(products, chosen[2], num_segments=NC + 1)
        return running[:NC]

    result = lax.map(position, jnp.arange(N_ROW * N_COL, dtype=jnp.int32))
    return result.reshape(N_ROW, N_COL, NC, BS, BS)
```

```python
import functools

import jax
import jax.numpy as jnp
from jax import lax
from jax.experimental import pallas as pl
from jax.experimental.pallas import tpu as pltpu
from jax.sharding import PartitionSpec as P

PARTS = 2
UNROLL = 34


def sort_lists(pairs, chunk_lanes, zero_block, block_count):
    slots = pairs.shape[1]
    a_row, b_row, c_row = pairs[0:1], pairs[1:2], pairs[2:3]
    iota = lambda shape, dim: lax.broadcasted_iota(jnp.int32, shape, dim)
    square = (slots, slots)
    c_across = jnp.broadcast_to(c_row, square)
    c_down = jnp.transpose(c_across)
    earlier = iota(square, 0) < iota(square, 1)
    rank = jnp.sum(jnp.where((c_down == c_across) & earlier, 1, 0), axis=0, keepdims=True)
    group = iota((block_count, slots), 0)
    c_short = jnp.broadcast_to(c_row, (block_count, slots))
    counts = jnp.sum(jnp.where(c_short == group, 1, 0), axis=1, keepdims=True)
    halves = jnp.broadcast_to((counts + 1) >> 1, (block_count, slots))
    before = jnp.sum(jnp.where(group < c_short, halves, 0), axis=0, keepdims=True)
    place = jnp.where(c_row < block_count, 2 * before + rank, 1023)
    first = jnp.where(rank == 0, 1, 0)
    word = place + (a_row << 10) + (b_row << 15) + (c_row << 22) + (first << 28)
    down = jnp.transpose(jnp.broadcast_to(word, square))
    if chunk_lanes != slots:
        down = down[:, :chunk_lanes]
    place = down & 1023
    entry = (((down >> 10) & 31) + 1) + (((down >> 15) & 127) << 8) + (((down >> 28) & 1) << 16)
    c_down = (down >> 22) & 63
    lane = iota((slots, chunk_lanes), 1)
    one = jnp.sum(jnp.where(place == 2 * lane, entry, 0), axis=0, keepdims=True)
    two = jnp.sum(jnp.where(place == 2 * lane + 1, entry, 0), axis=0, keepdims=True)
    last = jnp.max(jnp.where((c_down == lane) & (place < 1023), (place >> 1) + 1, 0), axis=0, keepdims=True)
    rows = []
    for picked in (one, two):
        a = picked & 255
        rows.append(jnp.where(a == 0, zero_block, a - 1))
    for picked in (one, two):
        rows.append((picked >> 8) & 255)
    rows.append(1 - ((one >> 16) & 1))
    rows.append(last)
    return rows


def kernel(
    pairs_ref,
    a_hbm,
    b_hbm,
    out_ref,
    *scratch,
    sizes,
):
    n_row, n_col, n_layer, ta, bs, nc, chunks, lanes, unroll = sizes
    rows = bs // PARTS
    scratch = list(scratch)

    def take(count):
        taken = scratch[:count]
        del scratch[:count]
        return taken

    a_bufs = [take(PARTS) for _ in range(3)]
    (b_buf, products) = take(2)
    plan_out = take(3)
    plan_in = take(2)
    plan_s = take(3)
    partial = [take(PARTS) for _ in range(3)]
    far_l = [take(PARTS) for _ in range(3)]
    far_r = [take(PARTS) for _ in range(3)]
    near_l = [take(PARTS) for _ in range(3)]
    near_r = [take(PARTS) for _ in range(3)]
    total = [take(PARTS) for _ in range(3)]
    shift = [take(PARTS) for _ in range(2)]
    local_sem, send_sem, recv_sem = take(3)

    r, q, l = lax.axis_index("row"), lax.axis_index("col"), lax.axis_index("layer")

    def at(dr=0, dq=0, dl=0):
        return {
            "row": lax.rem(r + dr + n_row, n_row),
            "col": lax.rem(q + dq + n_col, n_col),
            "layer": lax.rem(l + dl + n_layer, n_layer),
        }

    counter = [0]

    def send(src, dst, target):
        i = counter[0]
        counter[0] += 1
        copy = pltpu.make_async_remote_copy(
            src_ref=src,
            dst_ref=dst,
            send_sem=send_sem.at[i],
            recv_sem=recv_sem.at[i],
            device_id=target,
            device_id_type=pl.DeviceIdType.MESH,
        )
        copy.start()
        sent.append(copy)
        return copy

    sent = []
    local_counter = [0]

    def local(src, dst):
        i = local_counter[0]
        local_counter[0] += 1
        copy = pltpu.make_async_copy(src, dst, local_sem.at[i])
        copy.start()
        return copy

    nt = nc // n_layer
    half = nt // 2

    own_a = [
        local(a_hbm.at[:, pl.ds(m * rows, rows), :], a_bufs[0][m].at[pl.ds(0, ta)]) for m in range(PARTS)
    ]
    own_b = local(b_hbm, b_buf)

    barrier = pltpu.get_barrier_semaphore()
    partners = [at(1, -1), at(-1, 1), at(0, 1), at(0, -1), at(0, 2), at(0, -2), at(0, 0, 1), at(0, 0, -1)]
    for partner in partners:
        pl.semaphore_signal(barrier, inc=1, device_id=partner, device_id_type=pl.DeviceIdType.MESH)
    pl.semaphore_wait(barrier, len(partners))

    next_a = at(1, -1)
    hop1 = [
        send(
            a_hbm.at[:, pl.ds(m * rows, rows), :],
            a_bufs[1][m].at[pl.ds(0, ta)],
            next_a,
        )
        for m in range(PARTS)
    ]

    def forward(m):
        hop1[m].wait_recv()
        return send(a_bufs[1][m].at[pl.ds(0, ta)], a_bufs[2][m].at[pl.ds(0, ta)], next_a)

    plan_copy = [None] * 3
    for s in range(3):
        listed = sort_lists(pairs_ref[s], lanes, ta, nc)
        for i, row in enumerate(listed):
            plan_out[s][pl.ds(i, 1), :] = row
        plan_out[s][pl.ds(6, 2), :] = jnp.zeros((2, lanes), jnp.int32)
        if s == 0:
            plan_copy[0] = local(plan_out[0], plan_s[0])
        else:
            plan_copy[s] = send(plan_out[s], plan_in[s - 1], at(0, -s))

    for s in range(3):
        for m in range(PARTS):
            a_bufs[s][m][ta] = jnp.zeros((rows, bs), a_bufs[s][m].dtype)
    products[0] = jnp.zeros((rows, bs), jnp.float32)

    def compute(s, m):
        a_buf, plan, target = a_bufs[s][m], plan_s[s], partial[s][m]

        def one(k, running):
            left = jnp.concatenate([a_buf[plan[0, k]], a_buf[plan[1, k]]], axis=1)
            right = jnp.concatenate([b_buf[plan[2, k]], b_buf[plan[3, k]]], axis=0)
            product = jnp.dot(left, right, preferred_element_type=jnp.float32)
            running = jnp.where(plan[4, k] > 0, running, 0.0) + product
            products[k + 1] = running
            return running

        lax.fori_loop(0, chunks, one, jnp.zeros((rows, bs), jnp.float32), unroll=unroll)
        for c in range(nc):
            target[c] = products[plan[5, c]]

    right, left, across = at(0, 0, 1), at(0, 0, -1), at(0, 0, 2)
    right_at, left_at, across_at = nt * right["layer"], nt * left["layer"], nt * across["layer"]
    far_copies, plain_copies, summed_copies, shift_copies = {}, {}, {}, {}

    def spread(s, m):
        source = partial[s][m]
        far_copies[s, m] = (
            send(source.at[pl.ds(across_at, half)], far_l[s][m], right),
            send(source.at[pl.ds(across_at + half, half)], far_r[s][m], left),
        )
        plain_copies[s, m] = (
            send(source.at[pl.ds(right_at + half, half)], near_l[s][m].at[pl.ds(half, half)], right),
            send(source.at[pl.ds(left_at, half)], near_r[s][m].at[pl.ds(0, half)], left),
        )

    def relay(s, m):
        source = partial[s][m]
        from_left, from_right = far_copies[s, m]
        from_left.wait_recv()
        source[pl.ds(right_at, half)] = source[pl.ds(right_at, half)] + far_l[s][m][...]
        one = send(source.at[pl.ds(right_at, half)], near_l[s][m].at[pl.ds(0, half)], right)
        from_right.wait_recv()
        source[pl.ds(left_at + half, half)] = source[pl.ds(left_at + half, half)] + far_r[s][m][...]
        two = send(source.at[pl.ds(left_at + half, half)], near_r[s][m].at[pl.ds(half, half)], left)
        summed_copies[s, m] = (one, two)

    def collect(s, m):
        for copy in plain_copies[s, m] + summed_copies[s, m]:
            copy.wait_recv()
        own = partial[s][m][pl.ds(nt * l, nt)]
        total[s][m][...] = own + near_l[s][m][...] + near_r[s][m][...]
        if s:
            shift_copies[s, m] = send(total[s][m], shift[s - 1][m], at(0, s))

    def finish(m):
        for s in (1, 2):
            shift_copies[s, m].wait_recv()
        out_ref[:, pl.ds(m * rows, rows), :] = total[0][m][...] + shift[0][m][...] + shift[1][m][...]

    hop2 = [None] * PARTS
    own_b.wait()
    for copy in own_a:
        copy.wait()
    plan_copy[0].wait()
    compute(0, 0)
    spread(0, 0)
    hop2[0] = forward(0)
    compute(0, 1)
    spread(0, 1)
    plan_copy[1].wait_recv()
    plan_1 = local(plan_in[0], plan_s[1])
    plan_copy[2].wait_recv()
    plan_2 = local(plan_in[1], plan_s[2])
    relay(0, 0)
    plan_1.wait()
    plan_2.wait()
    compute(1, 0)
    spread(1, 0)
    relay(0, 1)
    collect(0, 0)
    hop2[1] = forward(1)
    compute(1, 1)
    spread(1, 1)
    relay(1, 0)
    collect(0, 1)
    hop2[0].wait_recv()
    compute(2, 0)
    spread(2, 0)
    relay(1, 1)
    collect(1, 0)
    relay(2, 0)
    collect(1, 1)
    hop2[1].wait_recv()
    compute(2, 1)
    spread(2, 1)
    collect(2, 0)
    relay(2, 1)
    finish(0)
    collect(2, 1)
    finish(1)
    for copy in sent:
        copy.wait_send()


def shards(left_panels, right_panels, pair_lists):
    left_own = left_panels[0, 0, 0]
    right_own = right_panels[0, 0, 0]
    pairs = pair_lists[0, 0, 0]
    ta, bs, _ = left_own.shape
    tb = right_own.shape[0]
    slots = pairs.shape[2]
    nc = 16
    n_row, n_col, n_layer = (lax.axis_size(axis) for axis in ("row", "col", "layer"))
    nt = nc // n_layer
    rows = bs // PARTS
    chunks = (slots + nc) // 2
    lanes = slots
    unroll = UNROLL if chunks % UNROLL == 0 else 2
    f32, i32, bf16 = jnp.float32, jnp.int32, left_own.dtype
    vmem = pltpu.VMEM
    scratch = [vmem((ta + 1, rows, bs), bf16) for _ in range(3 * PARTS)]
    scratch += [vmem((tb, bs, bs), bf16), vmem((chunks + 1, rows, bs), f32)]
    scratch += [vmem((8, lanes), i32) for _ in range(5)]
    scratch += [pltpu.SMEM((8, lanes), i32) for _ in range(3)]
    scratch += [vmem((nc, rows, bs), f32) for _ in range(3 * PARTS)]
    scratch += [vmem((nt // 2, rows, bs), f32) for _ in range(6 * PARTS)]
    scratch += [vmem((nt, rows, bs), f32) for _ in range(11 * PARTS)]
    copies = 2 * PARTS + 2 + 18 * PARTS + 2 * PARTS
    scratch += [pltpu.SemaphoreType.DMA((PARTS + 4,))]
    scratch += [pltpu.SemaphoreType.DMA((copies,)), pltpu.SemaphoreType.DMA((copies,))]
    sizes = (n_row, n_col, n_layer, ta, bs, nc, chunks, lanes, unroll)
    tiles = pl.pallas_call(
        functools.partial(kernel, sizes=sizes),
        out_shape=jax.ShapeDtypeStruct((nt, bs, bs), f32),
        in_specs=[
            pl.BlockSpec(memory_space=pltpu.VMEM),
            pl.BlockSpec(memory_space=pl.ANY),
            pl.BlockSpec(memory_space=pl.ANY),
        ],
        out_specs=pl.BlockSpec(memory_space=pltpu.VMEM),
        scratch_shapes=scratch,
        compiler_params=pltpu.CompilerParams(
            collective_id=0, has_side_effects=True, vmem_limit_bytes=40 * 2**20
        ),
        cost_estimate=pl.CostEstimate(flops=3 * slots * 2 * bs**3, bytes_accessed=3 * 2**20, transcendentals=0),
    )(pairs, left_own, right_own)
    return tiles[None, None]


def solution(mesh):
    placed = (
        P("row", "col", "layer", None, None, None),
        P("row", "col", "layer", None, None, None),
        P("row", "col", "layer", None, None, None),
    )
    return jax.shard_map(
        shards,
        mesh=mesh,
        in_specs=placed,
        out_specs=P("row", "col", "layer", None, None),
        check_vma=False,
    )
```

```python
import functools

import jax
import jax.numpy as jnp
from jax import lax
from jax.experimental import pallas as pl
from jax.experimental.pallas import tpu as pltpu
from jax.sharding import PartitionSpec as P

PARTS = ((64, 64), (64, 32, 32), (32, 32, 16, 16, 16, 16))
PIECES = (32, 32, 16, 16, 16, 16)
UNROLL = {128: 68, 64: 68, 48: 68, 32: 68, 16: 68}
DIRECT = ("11", "12", "20", "21", "22", "23", "24", "25")
SCHEDULE = (
    "o0", "c00", "o1", "q", "s00", "f0", "o2", "c01", "s01", "o3", "p", "c10", "s10", "f1", "c20", "f2",
    "s20", "r10", "f3", "o4", "o5", "c11", "s11", "c21", "s21", "k20", "c22", "k10", "f4", "c23", "s22", "k11",
    "f5", "s23", "c12", "k21", "s12", "c24", "k22", "c25", "s25", "s24", "r00", "k23", "k12", "r01", "k25", "k24",
    "k00", "k01", "z10", "z12", "z23", "z20", "z25", "z11", "z21", "z22", "z24",
)


def sort_lists(pairs, chunk_lanes, zero_block, block_count):
    a_row, b_row, c_row = pairs
    slots = c_row.shape[1]
    iota = lambda shape, dim: lax.broadcasted_iota(jnp.int32, shape, dim)
    square = (slots, slots)
    c_across = jnp.broadcast_to(c_row, square)
    c_down = jnp.transpose(c_across)
    earlier = iota(square, 0) < iota(square, 1)
    rank = jnp.sum(jnp.where((c_down == c_across) & earlier, 1, 0), axis=0, keepdims=True)
    group = iota((block_count, slots), 0)
    c_short = jnp.broadcast_to(c_row, (block_count, slots))
    counts = jnp.sum(jnp.where(c_short == group, 1, 0), axis=1, keepdims=True)
    halves = jnp.broadcast_to((counts + 1) >> 1, (block_count, slots))
    before = jnp.sum(jnp.where(group < c_short, halves, 0), axis=0, keepdims=True)
    place = jnp.where(c_row < block_count, 2 * before + rank, 1023)
    first = jnp.where(rank == 0, 1, 0)
    word = place + (a_row << 10) + (b_row << 15) + (c_row << 22) + (first << 28)
    down = jnp.transpose(jnp.broadcast_to(word, square))
    if chunk_lanes != slots:
        down = down[:, :chunk_lanes]
    place = down & 1023
    entry = (((down >> 10) & 31) + 1) + (((down >> 15) & 127) << 8) + (((down >> 28) & 1) << 16)
    c_down = (down >> 22) & 63
    lane = iota((slots, chunk_lanes), 1)
    one = jnp.sum(jnp.where(place == 2 * lane, entry, 0), axis=0, keepdims=True)
    two = jnp.sum(jnp.where(place == 2 * lane + 1, entry, 0), axis=0, keepdims=True)
    last = jnp.max(jnp.where((c_down == lane) & (place < 1023), (place >> 1) + 1, 0), axis=0, keepdims=True)
    rows = []
    for picked in (one, two):
        a = picked & 255
        rows.append(jnp.where(a == 0, zero_block, a - 1))
    for picked in (one, two):
        rows.append((picked >> 8) & 255)
    rows.append(1 - ((one >> 16) & 1))
    rows.append(last)
    return rows


def kernel(pairs_hbm, a_hbm, b_hbm, out_ref, *scratch, sizes):
    n_row, n_col, n_layer, ta, bs, nc, chunks, lanes, parts, pieces, unroll = sizes
    steps = len(parts)
    starts = lambda heights: [sum(heights[:m]) for m in range(len(heights))]
    offsets = [starts(heights) for heights in parts]
    piece_offsets = starts(pieces)
    scratch = list(scratch)

    def take(count):
        taken = scratch[:count]
        del scratch[:count]
        return taken

    def take_parts():
        return [take(len(heights)) for heights in parts]

    a_bufs = take_parts()
    b_buf, pairs_ref = take(2)
    heights_used = sorted({rows for heights in parts for rows in heights})
    products = dict(zip(heights_used, take(len(heights_used))))
    plan_out = take(steps)
    plan_in = take(steps - 1)
    plan_s = take(steps)
    partial, far, near_l, near_r, total, shift = (take_parts() for _ in range(6))
    local_sem, send_sem, recv_sem = take(3)

    r, q, l = lax.axis_index("row"), lax.axis_index("col"), lax.axis_index("layer")

    def at(dr=0, dq=0, dl=0):
        return {
            "row": lax.rem(r + dr + n_row, n_row),
            "col": lax.rem(q + dq + n_col, n_col),
            "layer": lax.rem(l + dl + n_layer, n_layer),
        }

    sent, started = [], []

    def send(src, dst, target):
        i = len(sent)
        copy = pltpu.make_async_remote_copy(
            src_ref=src,
            dst_ref=dst,
            send_sem=send_sem.at[i],
            recv_sem=recv_sem.at[i],
            device_id=target,
            device_id_type=pl.DeviceIdType.MESH,
        )
        copy.start()
        sent.append(copy)
        return copy

    def local(src, dst):
        copy = pltpu.make_async_copy(src, dst, local_sem.at[len(started)])
        copy.start()
        started.append(copy)
        return copy

    arrived = set()

    def arrive(copy):
        if id(copy) not in arrived:
            arrived.add(id(copy))
            copy.wait_recv()

    nt = nc // n_layer
    half = nt // 2

    own_pairs = local(pairs_hbm, pairs_ref)
    own_a = [
        local(a_hbm.at[:, pl.ds(offset, rows), :], buf.at[pl.ds(0, ta)])
        for offset, rows, buf in zip(offsets[0], parts[0], a_bufs[0])
    ]
    own_b = local(b_hbm, b_buf)

    barrier = pltpu.get_barrier_semaphore()
    partners = [at(1, -1), at(-1, 1), at(0, 1), at(0, -1), at(0, 2), at(0, -2)]
    partners += [at(0, 0, 1), at(0, 0, -1), at(0, 0, 2)]
    for partner in partners:
        pl.semaphore_signal(barrier, inc=1, device_id=partner, device_id_type=pl.DeviceIdType.MESH)
    pl.semaphore_wait(barrier, len(partners))

    next_a = at(1, -1)
    hop1, hop2 = {}, {}

    def members(s, m):
        low, high = offsets[s][m], offsets[s][m] + parts[s][m]
        return [i for i, offset in enumerate(piece_offsets) if low <= offset < high]

    def piece_of(s, i):
        for m in range(len(parts[s])):
            if i in members(s, m):
                return a_bufs[s][m].at[pl.ds(0, ta), pl.ds(piece_offsets[i] - offsets[s][m], pieces[i])]

    def begin(i):
        source = a_hbm.at[:, pl.ds(piece_offsets[i], pieces[i]), :]
        hop1[i] = send(source, piece_of(1, i), next_a)

    def forward(i):
        arrive(hop1[i])
        hop2[i] = send(piece_of(1, i), piece_of(2, i), next_a)

    order = list(SCHEDULE)
    while order[0][0] == "o":
        begin(int(order.pop(0)[1]))

    plan_copy = {}

    def list_step(s):
        listed = sort_lists([pairs_ref[s, i] for i in range(3)], lanes, ta, nc)
        for i, row in enumerate(listed):
            plan_out[s][pl.ds(i, 1), :] = row
        plan_out[s][pl.ds(6, 2), :] = jnp.zeros((2, lanes), jnp.int32)
        if s == 0:
            plan_copy[s] = local(plan_out[0], plan_s[0])
        else:
            plan_copy[s] = send(plan_out[s], plan_in[s - 1], at(0, -s))

    own_pairs.wait()
    list_step(0)

    for bufs in a_bufs:
        for buf in bufs:
            buf[ta] = jnp.zeros(buf.shape[1:], buf.dtype)
    for buf in products.values():
        buf[0] = jnp.zeros(buf.shape[1:], buf.dtype)

    def send_plans():
        for s in range(1, steps):
            list_step(s)

    def plans():
        for i in range(1, steps):
            arrive(plan_copy[i])
            plan_copy[i] = local(plan_in[i - 1], plan_s[i])

    waited = set()

    def once(copy):
        if id(copy) not in waited:
            waited.add(id(copy))
            copy.wait()

    def compute(s, m):
        once(plan_copy[s])
        if s == 0:
            once(own_b)
            once(own_a[m])
        else:
            for i in members(s, m):
                arrive((hop1, hop2)[s - 1][i])
        rows = parts[s][m]
        a_buf, plan, target, running_sums = a_bufs[s][m], plan_s[s], partial[s][m], products[rows]

        def one(k, running):
            left = jnp.concatenate([a_buf[plan[0, k]], a_buf[plan[1, k]]], axis=1)
            right = jnp.concatenate([b_buf[plan[2, k]], b_buf[plan[3, k]]], axis=0)
            product = jnp.dot(left, right, preferred_element_type=jnp.float32)
            running = jnp.where(plan[4, k] > 0, running, 0.0) + product
            running_sums[k + 1] = running
            return running

        lax.fori_loop(0, chunks, one, jnp.zeros((rows, bs), jnp.float32), unroll=unroll[rows])
        for c in range(nc):
            target[c] = running_sums[plan[5, c]]

    right, left, across = at(0, 0, 1), at(0, 0, -1), at(0, 0, 2)
    right_at, left_at, across_at = nt * right["layer"], nt * left["layer"], nt * across["layer"]
    far_copies, plain_copies, summed_copies, shift_copies = {}, {}, {}, {}

    def is_direct(s, m):
        return f"{s}{m}" in DIRECT

    def spread(s, m):
        source = partial[s][m]
        if is_direct(s, m):
            plain_copies[s, m] = (
                send(source.at[pl.ds(across_at, nt)], far[s][m], across),
                send(source.at[pl.ds(right_at, nt)], near_l[s][m], right),
                send(source.at[pl.ds(left_at, nt)], near_r[s][m], left),
            )
            return
        far_copies[s, m] = (
            send(source.at[pl.ds(across_at, half)], far[s][m].at[pl.ds(0, half)], right),
            send(source.at[pl.ds(across_at + half, half)], far[s][m].at[pl.ds(half, half)], left),
        )
        plain_copies[s, m] = (
            send(source.at[pl.ds(right_at + half, half)], near_l[s][m].at[pl.ds(half, half)], right),
            send(source.at[pl.ds(left_at, half)], near_r[s][m].at[pl.ds(0, half)], left),
        )

    def relay(s, m):
        source, passed = partial[s][m], far[s][m]
        from_left, from_right = far_copies[s, m]
        arrive(from_left)
        source[pl.ds(right_at, half)] = source[pl.ds(right_at, half)] + passed[pl.ds(0, half)]
        one = send(source.at[pl.ds(right_at, half)], near_l[s][m].at[pl.ds(0, half)], right)
        arrive(from_right)
        source[pl.ds(left_at + half, half)] = source[pl.ds(left_at + half, half)] + passed[pl.ds(half, half)]
        two = send(source.at[pl.ds(left_at + half, half)], near_r[s][m].at[pl.ds(half, half)], left)
        summed_copies[s, m] = (one, two)

    def collect(s, m):
        for copy in plain_copies[s, m] + summed_copies.get((s, m), ()):
            arrive(copy)
        summed = partial[s][m][pl.ds(nt * l, nt)] + near_l[s][m][...] + near_r[s][m][...]
        if is_direct(s, m):
            summed = summed + far[s][m][...]
        if s == 0:
            out_ref[:, pl.ds(offsets[s][m], parts[s][m]), :] = summed
        else:
            total[s][m][...] = summed
            shift_copies[s, m] = send(total[s][m], shift[s][m], at(0, s))

    def finish(s, m):
        arrive(shift_copies[s, m])
        rows = pl.ds(offsets[s][m], parts[s][m])
        out_ref[:, rows, :] = out_ref[:, rows, :] + shift[s][m][...]

    actions = {
        "o": begin,
        "f": forward,
        "c": compute,
        "s": spread,
        "r": relay,
        "k": collect,
        "z": finish,
        "p": plans,
        "q": send_plans,
    }
    for step in order:
        actions[step[0]](*(int(digit) for digit in step[1:]))
    for copy in sent:
        copy.wait_send()


def shards(left_panels, right_panels, pair_lists):
    left_own = left_panels[0, 0, 0]
    right_own = right_panels[0, 0, 0]
    pairs = pair_lists[0, 0, 0][:, :, None, :]
    ta, bs, _ = left_own.shape
    tb = right_own.shape[0]
    steps, _, _, slots = pairs.shape
    nc = 16
    n_row, n_col, n_layer = (lax.axis_size(axis) for axis in ("row", "col", "layer"))
    nt = nc // n_layer
    parts = tuple(tuple(rows * bs // 128 for rows in heights) for heights in PARTS)
    pieces = tuple(rows * bs // 128 for rows in PIECES)
    chunks = (slots + nc) // 2
    unroll = {rows * bs // 128: by if chunks % by == 0 else 2 for rows, by in UNROLL.items()}
    f32, i32, bf16 = jnp.float32, jnp.int32, left_own.dtype
    vmem = pltpu.VMEM
    every = [rows for heights in parts for rows in heights]
    scratch = [vmem((ta + 1, rows, bs), bf16) for rows in every]
    scratch += [vmem((tb, bs, bs), bf16), vmem(pairs.shape, i32)]
    scratch += [vmem((chunks + 1, rows, bs), f32) for rows in sorted(set(every))]
    scratch += [vmem((8, slots), i32) for _ in range(2 * steps - 1)]
    scratch += [pltpu.SMEM((8, slots), i32) for _ in range(steps)]
    for blocks in (nc, nt, nt, nt, nt, nt):
        scratch += [vmem((blocks, rows, bs), f32) for rows in every]
    copies = 2 * len(pieces) + 2 + 7 * len(every)
    scratch += [pltpu.SemaphoreType.DMA((len(parts[0]) + 5,))]
    scratch += [pltpu.SemaphoreType.DMA((copies,)), pltpu.SemaphoreType.DMA((copies,))]
    sizes = (n_row, n_col, n_layer, ta, bs, nc, chunks, slots, parts, pieces, unroll)
    tiles = pl.pallas_call(
        functools.partial(kernel, sizes=sizes),
        out_shape=jax.ShapeDtypeStruct((nt, bs, bs), f32),
        in_specs=[
            pl.BlockSpec(memory_space=pltpu.HBM),
            pl.BlockSpec(memory_space=pltpu.HBM),
            pl.BlockSpec(memory_space=pltpu.HBM),
        ],
        out_specs=pl.BlockSpec(memory_space=pltpu.VMEM),
        scratch_shapes=scratch,
        compiler_params=pltpu.CompilerParams(
            collective_id=0, has_side_effects=True, vmem_limit_bytes=50 * 2**20
        ),
        cost_estimate=pl.CostEstimate(flops=3 * slots * 2 * bs**3, bytes_accessed=3 * 2**20, transcendentals=0),
    )(*(pltpu.with_memory_space_constraint(x, pltpu.HBM) for x in (pairs, left_own, right_own)))
    return tiles[None, None]


def solution(mesh):
    placed = (
        P("row", "col", "layer", None, None, None),
        P("row", "col", "layer", None, None, None),
        P("row", "col", "layer", None, None, None),
    )
    return jax.shard_map(
        shards,
        mesh=mesh,
        in_specs=placed,
        out_specs=P("row", "col", "layer", None, None),
        check_vma=False,
    )
```

```python
import functools

import jax
import jax.numpy as jnp
from jax import lax
from jax.experimental import pallas as pl
from jax.experimental.pallas import tpu as pltpu
from jax.sharding import PartitionSpec as P

PARTS = ((64, 64), (64, 32, 32), (32, 32, 16, 16, 16, 16))
PIECES = (32, 32, 16, 16, 16, 16)
UNROLL = {128: 68, 64: 68, 48: 68, 32: 68, 16: 68}
DIRECT = ("11", "12", "20", "21", "22", "23", "24", "25")
SCHEDULE = (
    "o0", "c00", "o1", "q", "s00", "f0", "o2", "c01", "s01", "o3", "p", "c10", "s10", "f1", "c20", "f2",
    "s20", "r10", "f3", "o4", "o5", "c11", "s11", "c21", "s21", "k20", "c22", "k10", "f4", "c23", "s22", "k11",
    "f5", "s23", "c12", "k21", "s12", "c24", "k22", "c25", "s25", "s24", "r00", "k23", "k12", "r01", "k25", "k24",
    "k00", "k01", "z10", "z12", "z23", "z20", "z25", "z11", "z21", "z22", "z24",
)


def sort_lists(pairs, chunk_lanes, zero_block, block_count):
    a_row, b_row, c_row = pairs
    slots = c_row.shape[1]
    iota = lambda shape, dim: lax.broadcasted_iota(jnp.int32, shape, dim)
    square = (slots, slots)
    c_across = jnp.broadcast_to(c_row, square)
    c_down = jnp.transpose(c_across)
    earlier = iota(square, 0) < iota(square, 1)
    rank = jnp.sum(jnp.where((c_down == c_across) & earlier, 1, 0), axis=0, keepdims=True)
    group = iota((block_count, slots), 0)
    c_short = jnp.broadcast_to(c_row, (block_count, slots))
    counts = jnp.sum(jnp.where(c_short == group, 1, 0), axis=1, keepdims=True)
    halves = jnp.broadcast_to((counts + 1) >> 1, (block_count, slots))
    before = jnp.sum(jnp.where(group < c_short, halves, 0), axis=0, keepdims=True)
    place = jnp.where(c_row < block_count, 2 * before + rank, 1023)
    first = jnp.where(rank == 0, 1, 0)
    word = place + (a_row << 10) + (b_row << 15) + (c_row << 22) + (first << 28)
    down = jnp.transpose(jnp.broadcast_to(word, square))
    if chunk_lanes != slots:
        down = down[:, :chunk_lanes]
    place = down & 1023
    entry = (((down >> 10) & 31) + 1) + (((down >> 15) & 127) << 8) + (((down >> 28) & 1) << 16)
    c_down = (down >> 22) & 63
    lane = iota((slots, chunk_lanes), 1)
    one = jnp.sum(jnp.where(place == 2 * lane, entry, 0), axis=0, keepdims=True)
    two = jnp.sum(jnp.where(place == 2 * lane + 1, entry, 0), axis=0, keepdims=True)
    last = jnp.max(jnp.where((c_down == lane) & (place < 1023), (place >> 1) + 1, 0), axis=0, keepdims=True)
    rows = []
    for picked in (one, two):
        a = picked & 255
        rows.append(jnp.where(a == 0, zero_block, a - 1))
    for picked in (one, two):
        rows.append((picked >> 8) & 255)
    rows.append(1 - ((one >> 16) & 1))
    rows.append(last)
    return rows


def kernel(pairs_hbm, a_hbm, b_hbm, out_ref, *scratch, sizes):
    n_row, n_col, n_layer, ta, bs, nc, chunks, lanes, parts, pieces, unroll = sizes
    steps = len(parts)
    starts = lambda heights: [sum(heights[:m]) for m in range(len(heights))]
    offsets = [starts(heights) for heights in parts]
    piece_offsets = starts(pieces)
    scratch = list(scratch)

    def take(count):
        taken = scratch[:count]
        del scratch[:count]
        return taken

    def take_parts():
        return [take(len(heights)) for heights in parts]

    a_bufs = take_parts()
    b_buf, pairs_ref = take(2)
    heights_used = sorted({rows for heights in parts for rows in heights})
    products = dict(zip(heights_used, take(len(heights_used))))
    plan_out = take(steps)
    plan_in = take(steps - 1)
    plan_s = take(steps)
    partial, inbox, total, shift = (take_parts() for _ in range(4))
    local_sem, send_sem, recv_sem = take(3)

    r, q, l = lax.axis_index("row"), lax.axis_index("col"), lax.axis_index("layer")

    def at(dr=0, dq=0, dl=0):
        return {
            "row": lax.rem(r + dr + n_row, n_row),
            "col": lax.rem(q + dq + n_col, n_col),
            "layer": lax.rem(l + dl + n_layer, n_layer),
        }

    started = []
    send_slots, recv_slots = {}, {}

    def send_slot(key):
        return send_sem.at[send_slots.setdefault(key, len(send_slots))]

    def recv_slot(key):
        return recv_sem.at[recv_slots.setdefault(key, len(recv_slots))]

    def send(src, dst, target, send_key, recv_key):
        copy = pltpu.make_async_remote_copy(
            src_ref=src,
            dst_ref=dst,
            send_sem=send_slot(send_key),
            recv_sem=recv_slot(recv_key),
            device_id=target,
            device_id_type=pl.DeviceIdType.MESH,
        )
        copy.start()
        return copy

    def wait_bytes(ref, sem):
        pltpu.make_async_copy(ref, ref, sem).wait()

    def local(src, dst):
        copy = pltpu.make_async_copy(src, dst, local_sem.at[len(started)])
        copy.start()
        started.append(copy)
        return copy

    arrived = set()

    def arrive(copy):
        if id(copy) not in arrived:
            arrived.add(id(copy))
            copy.wait_recv()

    nt = nc // n_layer
    half = nt // 2

    barrier = pltpu.get_barrier_semaphore()
    partners = [at(0, 2), at(0, -2), at(-1, 1), at(1, -1), at(0, 1), at(0, -1)]
    partners += [at(0, 0, 1), at(0, 0, -1), at(0, 0, 2)]
    for partner in partners:
        pl.semaphore_signal(barrier, inc=1, device_id=partner, device_id_type=pl.DeviceIdType.MESH)
    own_pairs = local(pairs_hbm, pairs_ref)
    own_a = [
        local(a_hbm.at[:, pl.ds(offset, rows), :], buf.at[pl.ds(0, ta)])
        for offset, rows, buf in zip(offsets[0], parts[0], a_bufs[0])
    ]
    own_b = local(b_hbm, b_buf)

    pl.semaphore_wait(barrier, len(partners))

    next_a = at(1, -1)
    hop1, hop2 = {}, {}

    waited = set()

    def once(copy):
        if id(copy) not in waited:
            waited.add(id(copy))
            copy.wait()

    def members(s, m):
        low, high = offsets[s][m], offsets[s][m] + parts[s][m]
        return [i for i, offset in enumerate(piece_offsets) if low <= offset < high]

    def piece_of(s, i):
        for m in range(len(parts[s])):
            if i in members(s, m):
                return a_bufs[s][m].at[pl.ds(0, ta), pl.ds(piece_offsets[i] - offsets[s][m], pieces[i])]

    def begin(i):
        for m, offset in enumerate(offsets[0]):
            if offset <= piece_offsets[i] < offset + parts[0][m]:
                once(own_a[m])
        hop1[i] = send(piece_of(0, i), piece_of(1, i), next_a, "own", ("first", i))

    def forward(i):
        arrive(hop1[i])
        hop2[i] = send(piece_of(1, i), piece_of(2, i), next_a, "passed", ("second", i))

    order = list(SCHEDULE)
    while order[0][0] == "o":
        begin(int(order.pop(0)[1]))

    plan_copy = {}

    def list_step(s):
        listed = sort_lists([pairs_ref[s, i] for i in range(3)], lanes, ta, nc)
        for i, row in enumerate(listed):
            plan_out[s][pl.ds(i, 1), :] = row
        plan_out[s][pl.ds(6, 2), :] = jnp.zeros((2, lanes), jnp.int32)
        if s == 0:
            plan_copy[s] = local(plan_out[0], plan_s[0])
        else:
            plan_copy[s] = send(plan_out[s], plan_in[s - 1], at(0, -s), ("plan", s), ("plan", s))

    own_pairs.wait()
    list_step(0)

    for bufs in a_bufs:
        for buf in bufs:
            buf[ta] = jnp.zeros(buf.shape[1:], buf.dtype)
    for buf in products.values():
        buf[0] = jnp.zeros(buf.shape[1:], buf.dtype)

    def send_plans():
        for s in range(1, steps):
            list_step(s)

    plan_sends = []

    def plans():
        for i in range(1, steps):
            arrive(plan_copy[i])
            plan_sends.append(plan_copy[i])
            plan_copy[i] = local(plan_in[i - 1], plan_s[i])

    def compute(s, m):
        once(plan_copy[s])
        if s == 0:
            once(own_b)
            once(own_a[m])
        else:
            for i in members(s, m):
                arrive((hop1, hop2)[s - 1][i])
        rows = parts[s][m]
        a_buf, plan, target, running_sums = a_bufs[s][m], plan_s[s], partial[s][m], products[rows]

        def one(k, running):
            left = jnp.concatenate([a_buf[plan[0, k]], a_buf[plan[1, k]]], axis=1)
            right = jnp.concatenate([b_buf[plan[2, k]], b_buf[plan[3, k]]], axis=0)
            product = jnp.dot(left, right, preferred_element_type=jnp.float32)
            running = jnp.where(plan[4, k] > 0, running, 0.0) + product
            running_sums[k + 1] = running
            return running

        lax.fori_loop(0, chunks, one, jnp.zeros((rows, bs), jnp.float32), unroll=unroll[rows])
        for c in range(nc):
            target[c] = running_sums[plan[5, c]]

    right, left, across = at(0, 0, 1), at(0, 0, -1), at(0, 0, 2)
    right_at, left_at, across_at = nt * right["layer"], nt * left["layer"], nt * across["layer"]
    shift_copies = {}

    def is_direct(s, m):
        return f"{s}{m}" in DIRECT

    def spread(s, m):
        source, box = partial[s][m], inbox[s][m]

        def pass_on(start, count, slot, target, kind="all"):
            send(source.at[pl.ds(start, count)], box.at[pl.ds(slot, count)], target, (s, m), (kind, s, m))

        if is_direct(s, m):
            pass_on(across_at, nt, 0, across)
            pass_on(right_at, nt, nt, right)
            pass_on(left_at, nt, 2 * nt, left)
            return
        pass_on(across_at, half, 0, right, "far")
        pass_on(across_at + half, half, half, left, "far")
        pass_on(right_at + half, half, nt + half, right)
        pass_on(left_at, half, 2 * nt, left)

    def relay(s, m):
        source, box = partial[s][m], inbox[s][m]
        wait_bytes(box.at[pl.ds(0, nt)], recv_slot(("far", s, m)))
        for start, slot, place, target in ((right_at, 0, nt, right), (left_at + half, half, 2 * nt + half, left)):
            blocks = pl.ds(start, half)
            source[blocks] = source[blocks] + box[pl.ds(slot, half)]
            send(source.at[blocks], box.at[pl.ds(place, half)], target, (s, m), ("all", s, m))

    def collect(s, m):
        box, sem = inbox[s][m], recv_slot(("all", s, m))
        summed = partial[s][m][pl.ds(nt * l, nt)]
        if is_direct(s, m):
            wait_bytes(box, sem)
            summed = summed + box[pl.ds(0, nt)]
        else:
            wait_bytes(box.at[pl.ds(nt, 2 * nt)], sem)
        summed = summed + box[pl.ds(nt, nt)] + box[pl.ds(2 * nt, nt)]
        if s == 0:
            out_ref[:, pl.ds(offsets[s][m], parts[s][m]), :] = summed
        else:
            total[s][m][...] = summed
            shift_copies[s, m] = send(total[s][m], shift[s][m], at(0, s), (s, m), ("shift", s, m))

    def finish(s, m):
        arrive(shift_copies[s, m])
        rows = pl.ds(offsets[s][m], parts[s][m])
        out_ref[:, rows, :] = out_ref[:, rows, :] + shift[s][m][...]

    actions = {
        "o": begin,
        "f": forward,
        "c": compute,
        "s": spread,
        "r": relay,
        "k": collect,
        "z": finish,
        "p": plans,
        "q": send_plans,
    }
    for step in order:
        actions[step[0]](*(int(digit) for digit in step[1:]))
    for s in range(steps):
        for m, source in enumerate(partial[s]):
            wait_bytes(source.at[pl.ds(0, 3 * nt + (nt if s else 0))], send_slot((s, m)))
    for key in ("own", "passed"):
        wait_bytes(b_buf.at[pl.ds(0, ta)], send_slot(key))
    for copy in plan_sends:
        copy.wait_send()


def shards(left_panels, right_panels, pair_lists):
    left_own = left_panels[0, 0, 0]
    right_own = right_panels[0, 0, 0]
    pairs = pair_lists[0, 0, 0][:, :, None, :]
    ta, bs, _ = left_own.shape
    tb = right_own.shape[0]
    steps, _, _, slots = pairs.shape
    nc = 16
    n_row, n_col, n_layer = (lax.axis_size(axis) for axis in ("row", "col", "layer"))
    nt = nc // n_layer
    parts = tuple(tuple(rows * bs // 128 for rows in heights) for heights in PARTS)
    pieces = tuple(rows * bs // 128 for rows in PIECES)
    chunks = (slots + nc) // 2
    unroll = {rows * bs // 128: by if chunks % by == 0 else 2 for rows, by in UNROLL.items()}
    f32, i32, bf16 = jnp.float32, jnp.int32, left_own.dtype
    vmem = pltpu.VMEM
    every = [rows for heights in parts for rows in heights]
    scratch = [vmem((ta + 1, rows, bs), bf16) for rows in every]
    scratch += [vmem((tb, bs, bs), bf16), vmem(pairs.shape, i32)]
    scratch += [vmem((chunks + 1, rows, bs), f32) for rows in sorted(set(every))]
    scratch += [vmem((8, slots), i32) for _ in range(2 * steps - 1)]
    scratch += [pltpu.SMEM((8, slots), i32) for _ in range(steps)]
    for blocks in (nc, 3 * nt, nt, nt):
        scratch += [vmem((blocks, rows, bs), f32) for rows in every]
    sends = len(every) + 2 + steps - 1
    receives = 2 * len(pieces) + steps - 1 + 3 * len(every) - len(DIRECT) - len(parts[0])
    scratch += [pltpu.SemaphoreType.DMA((len(parts[0]) + steps + 2,))]
    scratch += [pltpu.SemaphoreType.DMA((sends,)), pltpu.SemaphoreType.DMA((receives,))]
    sizes = (n_row, n_col, n_layer, ta, bs, nc, chunks, slots, parts, pieces, unroll)
    tiles = pl.pallas_call(
        functools.partial(kernel, sizes=sizes),
        out_shape=jax.ShapeDtypeStruct((nt, bs, bs), f32),
        in_specs=[
            pl.BlockSpec(memory_space=pltpu.HBM),
            pl.BlockSpec(memory_space=pltpu.HBM),
            pl.BlockSpec(memory_space=pltpu.HBM),
        ],
        out_specs=pl.BlockSpec(memory_space=pltpu.VMEM),
        scratch_shapes=scratch,
        compiler_params=pltpu.CompilerParams(
            collective_id=0, has_side_effects=True, vmem_limit_bytes=50 * 2**20
        ),
        cost_estimate=pl.CostEstimate(flops=3 * slots * 2 * bs**3, bytes_accessed=3 * 2**20, transcendentals=0),
    )(*(pltpu.with_memory_space_constraint(x, pltpu.HBM) for x in (pairs, left_own, right_own)))
    return tiles[None, None]


def solution(mesh):
    placed = (
        P("row", "col", "layer", None, None, None),
        P("row", "col", "layer", None, None, None),
        P("row", "col", "layer", None, None, None),
    )
    return jax.shard_map(
        shards,
        mesh=mesh,
        in_specs=placed,
        out_specs=P("row", "col", "layer", None, None),
        check_vma=False,
    )
```

```python
import functools

import jax
import jax.numpy as jnp
from jax import lax
from jax.experimental import pallas as pl
from jax.experimental.pallas import tpu as pltpu
from jax.sharding import PartitionSpec as P

PARTS = ((64, 64), (64, 32, 32), (32, 32, 16, 16, 16, 16))
PIECES = (32, 32, 16, 16, 16, 16)
UNROLL = {128: 68, 64: 68, 48: 68, 32: 68, 16: 68}
DIRECT = ("11", "12", "20", "21", "22", "23", "24", "25")
SCHEDULE = (
    "o0", "c00", "o1", "q", "s00", "c01", "f0", "s01", "o2", "o3", "p", "c10", "s10", "f1", "c20", "s20",
    "f2", "o4", "f3", "o5", "r10", "c11", "s11", "c21", "k20", "s21", "c22", "f4", "s22", "k10", "c23", "f5",
    "k11", "s23", "c12", "k21", "s12", "c24", "k22", "s24", "k23", "c25", "s25", "r00", "k12", "r01", "k24", "k25",
    "k00", "k01", "z21", "z12", "z24", "z20", "z23", "z11", "z22", "z10", "z25",
)


def sort_lists(pairs, chunk_lanes, zero_block, block_count):
    a_row, b_row, c_row = pairs
    slots = c_row.shape[1]
    iota = lambda shape, dim: lax.broadcasted_iota(jnp.int32, shape, dim)
    square = (slots, slots)
    c_across = jnp.broadcast_to(c_row, square)
    c_down = jnp.transpose(c_across)
    earlier = iota(square, 0) < iota(square, 1)
    rank = jnp.sum(jnp.where((c_down == c_across) & earlier, 1, 0), axis=0, keepdims=True)
    group = iota((block_count, slots), 0)
    c_short = jnp.broadcast_to(c_row, (block_count, slots))
    counts = jnp.sum(jnp.where(c_short == group, 1, 0), axis=1, keepdims=True)
    halves = jnp.broadcast_to((counts + 1) >> 1, (block_count, slots))
    before = jnp.sum(jnp.where(group < c_short, halves, 0), axis=0, keepdims=True)
    place = jnp.where(c_row < block_count, 2 * before + rank, 1023)
    first = jnp.where(rank == 0, 1, 0)
    word = place + (a_row << 10) + (b_row << 15) + (c_row << 22) + (first << 28)
    down = jnp.transpose(jnp.broadcast_to(word, square))
    if chunk_lanes != slots:
        down = down[:, :chunk_lanes]
    place = down & 1023
    entry = (((down >> 10) & 31) + 1) + (((down >> 15) & 127) << 8) + (((down >> 28) & 1) << 16)
    c_down = (down >> 22) & 63
    lane = iota((slots, chunk_lanes), 1)
    one = jnp.sum(jnp.where(place == 2 * lane, entry, 0), axis=0, keepdims=True)
    two = jnp.sum(jnp.where(place == 2 * lane + 1, entry, 0), axis=0, keepdims=True)
    last = jnp.max(jnp.where((c_down == lane) & (place < 1023), (place >> 1) + 1, 0), axis=0, keepdims=True)
    rows = []
    for picked in (one, two):
        a = picked & 255
        rows.append(jnp.where(a == 0, zero_block, a - 1))
    for picked in (one, two):
        rows.append((picked >> 8) & 255)
    rows.append(1 - ((one >> 16) & 1))
    rows.append(last)
    return rows


def kernel(pairs_hbm, a_hbm, b_hbm, out_ref, *scratch, sizes):
    n_row, n_col, n_layer, ta, bs, nc, chunks, lanes, parts, pieces, unroll = sizes
    steps = len(parts)
    starts = lambda heights: [sum(heights[:m]) for m in range(len(heights))]
    offsets = [starts(heights) for heights in parts]
    piece_offsets = starts(pieces)
    scratch = list(scratch)

    def take(count):
        taken = scratch[:count]
        del scratch[:count]
        return taken

    def take_parts():
        return [take(len(heights)) for heights in parts]

    a_bufs = take_parts()
    b_buf, pairs_ref = take(2)
    heights_used = sorted({rows for heights in parts for rows in heights})
    products = dict(zip(heights_used, take(len(heights_used))))
    plan_out = take(steps)
    plan_in = take(steps - 1)
    plan_s = take(steps)
    partial, inbox, total, shift = (take_parts() for _ in range(4))
    local_sem, send_sem, recv_sem = take(3)

    r, q, l = lax.axis_index("row"), lax.axis_index("col"), lax.axis_index("layer")

    def at(dr=0, dq=0, dl=0):
        return {
            "row": lax.rem(r + dr + n_row, n_row),
            "col": lax.rem(q + dq + n_col, n_col),
            "layer": lax.rem(l + dl + n_layer, n_layer),
        }

    started = []
    send_slots, recv_slots = {}, {}

    def send_slot(key):
        return send_sem.at[send_slots.setdefault(key, len(send_slots))]

    def recv_slot(key):
        return recv_sem.at[recv_slots.setdefault(key, len(recv_slots))]

    def send(src, dst, target, send_key, recv_key):
        copy = pltpu.make_async_remote_copy(
            src_ref=src,
            dst_ref=dst,
            send_sem=send_slot(send_key),
            recv_sem=recv_slot(recv_key),
            device_id=target,
            device_id_type=pl.DeviceIdType.MESH,
        )
        copy.start()
        return copy

    def wait_bytes(ref, sem):
        pltpu.make_async_copy(ref, ref, sem).wait()

    def local(src, dst):
        copy = pltpu.make_async_copy(src, dst, local_sem.at[len(started)])
        copy.start()
        started.append(copy)
        return copy

    arrived = set()

    def arrive(copy):
        if id(copy) not in arrived:
            arrived.add(id(copy))
            copy.wait_recv()

    nt = nc // n_layer
    half = nt // 2

    barrier = pltpu.get_barrier_semaphore()
    partners = [at(0, 2), at(0, -2), at(-1, 1), at(1, -1), at(0, 1), at(0, -1)]
    partners += [at(0, 0, 1), at(0, 0, -1), at(0, 0, 2)]
    for partner in partners:
        pl.semaphore_signal(barrier, inc=1, device_id=partner, device_id_type=pl.DeviceIdType.MESH)
    own_pairs = local(pairs_hbm, pairs_ref)
    own_a = [
        local(a_hbm.at[:, pl.ds(offset, rows), :], buf.at[pl.ds(0, ta)])
        for offset, rows, buf in zip(offsets[0], parts[0], a_bufs[0])
    ]
    own_b = local(b_hbm, b_buf)

    pl.semaphore_wait(barrier, len(partners))

    next_a = at(1, -1)
    hop1, hop2 = {}, {}

    waited = set()

    def once(copy):
        if id(copy) not in waited:
            waited.add(id(copy))
            copy.wait()

    def members(s, m):
        low, high = offsets[s][m], offsets[s][m] + parts[s][m]
        return [i for i, offset in enumerate(piece_offsets) if low <= offset < high]

    def piece_of(s, i):
        for m in range(len(parts[s])):
            if i in members(s, m):
                return a_bufs[s][m].at[pl.ds(0, ta), pl.ds(piece_offsets[i] - offsets[s][m], pieces[i])]

    def begin(i):
        for m, offset in enumerate(offsets[0]):
            if offset <= piece_offsets[i] < offset + parts[0][m]:
                once(own_a[m])
        hop1[i] = send(piece_of(0, i), piece_of(1, i), next_a, "a", ("first", i))

    def forward(i):
        arrive(hop1[i])
        hop2[i] = send(piece_of(1, i), piece_of(2, i), next_a, "a", ("second", i))

    order = list(SCHEDULE)
    while order[0][0] == "o":
        begin(int(order.pop(0)[1]))

    plan_copy = {}

    def list_step(s):
        listed = sort_lists([pairs_ref[s, i] for i in range(3)], lanes, ta, nc)
        for i, row in enumerate(listed):
            plan_out[s][pl.ds(i, 1), :] = row
        plan_out[s][pl.ds(6, 2), :] = jnp.zeros((2, lanes), jnp.int32)
        if s == 0:
            plan_copy[s] = local(plan_out[0], plan_s[0])
        else:
            plan_copy[s] = send(plan_out[s], plan_in[s - 1], at(0, -s), ("plan", s), ("plan", s))

    own_pairs.wait()
    list_step(0)

    for bufs in a_bufs:
        for buf in bufs:
            buf[ta] = jnp.zeros(buf.shape[1:], buf.dtype)
    for buf in products.values():
        buf[0] = jnp.zeros(buf.shape[1:], buf.dtype)

    def send_plans():
        for s in range(1, steps):
            list_step(s)

    plan_sends = []

    def plans():
        for i in range(1, steps):
            arrive(plan_copy[i])
            plan_sends.append(plan_copy[i])
            plan_copy[i] = local(plan_in[i - 1], plan_s[i])

    def compute(s, m):
        once(plan_copy[s])
        if s == 0:
            once(own_b)
            once(own_a[m])
        else:
            for i in members(s, m):
                arrive((hop1, hop2)[s - 1][i])
        rows = parts[s][m]
        a_buf, plan, target, running_sums = a_bufs[s][m], plan_s[s], partial[s][m], products[rows]

        def one(k, running):
            left = jnp.concatenate([a_buf[plan[0, k]], a_buf[plan[1, k]]], axis=1)
            right = jnp.concatenate([b_buf[plan[2, k]], b_buf[plan[3, k]]], axis=0)
            product = jnp.dot(left, right, preferred_element_type=jnp.float32)
            running = jnp.where(plan[4, k] > 0, running, 0.0) + product
            running_sums[k + 1] = running
            return running

        lax.fori_loop(0, chunks, one, jnp.zeros((rows, bs), jnp.float32), unroll=unroll[rows])
        for c in range(nc):
            target[c] = running_sums[plan[5, c]]

    right, left, across = at(0, 0, 1), at(0, 0, -1), at(0, 0, 2)
    right_at, left_at, across_at = nt * right["layer"], nt * left["layer"], nt * across["layer"]
    shift_copies = {}

    def is_direct(s, m):
        return f"{s}{m}" in DIRECT

    def spread(s, m):
        source, box = partial[s][m], inbox[s][m]

        def pass_on(start, count, slot, target, kind="all"):
            send(source.at[pl.ds(start, count)], box.at[pl.ds(slot, count)], target, s, (kind, s, m))

        if is_direct(s, m):
            pass_on(across_at, nt, 0, across)
            pass_on(right_at, nt, nt, right)
            pass_on(left_at, nt, 2 * nt, left)
            return
        pass_on(across_at, half, 0, right, "far")
        pass_on(across_at + half, half, half, left, "far")
        pass_on(right_at + half, half, nt + half, right)
        pass_on(left_at, half, 2 * nt, left)

    def relay(s, m):
        source, box = partial[s][m], inbox[s][m]
        wait_bytes(box.at[pl.ds(0, nt)], recv_slot(("far", s, m)))
        for start, slot, place, target in ((right_at, 0, nt, right), (left_at + half, half, 2 * nt + half, left)):
            blocks = pl.ds(start, half)
            source[blocks] = source[blocks] + box[pl.ds(slot, half)]
            send(source.at[blocks], box.at[pl.ds(place, half)], target, s, ("all", s, m))

    def collect(s, m):
        box, sem = inbox[s][m], recv_slot(("all", s, m))
        summed = partial[s][m][pl.ds(nt * l, nt)]
        if is_direct(s, m):
            wait_bytes(box, sem)
            summed = summed + box[pl.ds(0, nt)]
        else:
            wait_bytes(box.at[pl.ds(nt, 2 * nt)], sem)
        summed = summed + box[pl.ds(nt, nt)] + box[pl.ds(2 * nt, nt)]
        if s == 0:
            out_ref[:, pl.ds(offsets[s][m], parts[s][m]), :] = summed
        else:
            total[s][m][...] = summed
            shift_copies[s, m] = send(total[s][m], shift[s][m], at(0, s), s, ("shift", s, m))

    def finish(s, m):
        arrive(shift_copies[s, m])
        rows = pl.ds(offsets[s][m], parts[s][m])
        out_ref[:, rows, :] = out_ref[:, rows, :] + shift[s][m][...]

    actions = {
        "o": begin,
        "f": forward,
        "c": compute,
        "s": spread,
        "r": relay,
        "k": collect,
        "z": finish,
        "p": plans,
        "q": send_plans,
    }
    for step in order:
        actions[step[0]](*(int(digit) for digit in step[1:]))
    for s in range(steps):
        blocks = 3 * nt + (nt if s else 0)
        wait_bytes(b_buf.at[pl.ds(0, 2 * blocks)], send_slot(s))
    wait_bytes(b_buf.at[pl.ds(0, 2 * ta)], send_slot("a"))
    for copy in plan_sends:
        copy.wait_send()


def shards(left_panels, right_panels, pair_lists):
    left_own = left_panels[0, 0, 0]
    right_own = right_panels[0, 0, 0]
    pairs = pair_lists[0, 0, 0][:, :, None, :]
    ta, bs, _ = left_own.shape
    tb = right_own.shape[0]
    steps, _, _, slots = pairs.shape
    nc = 16
    n_row, n_col, n_layer = (lax.axis_size(axis) for axis in ("row", "col", "layer"))
    nt = nc // n_layer
    parts = tuple(tuple(rows * bs // 128 for rows in heights) for heights in PARTS)
    pieces = tuple(rows * bs // 128 for rows in PIECES)
    chunks = (slots + nc) // 2
    unroll = {rows * bs // 128: by if chunks % by == 0 else 2 for rows, by in UNROLL.items()}
    f32, i32, bf16 = jnp.float32, jnp.int32, left_own.dtype
    vmem = pltpu.VMEM
    every = [rows for heights in parts for rows in heights]
    scratch = [vmem((ta + 1, rows, bs), bf16) for rows in every]
    scratch += [vmem((tb, bs, bs), bf16), vmem(pairs.shape, i32)]
    scratch += [vmem((chunks + 1, rows, bs), f32) for rows in sorted(set(every))]
    scratch += [vmem((8, slots), i32) for _ in range(2 * steps - 1)]
    scratch += [pltpu.SMEM((8, slots), i32) for _ in range(steps)]
    for blocks in (nc, 3 * nt, nt, nt):
        scratch += [vmem((blocks, rows, bs), f32) for rows in every]
    sends = steps + 1 + steps - 1
    receives = 2 * len(pieces) + steps - 1 + 3 * len(every) - len(DIRECT) - len(parts[0])
    scratch += [pltpu.SemaphoreType.DMA((len(parts[0]) + steps + 2,))]
    scratch += [pltpu.SemaphoreType.DMA((sends,)), pltpu.SemaphoreType.DMA((receives,))]
    sizes = (n_row, n_col, n_layer, ta, bs, nc, chunks, slots, parts, pieces, unroll)
    tiles = pl.pallas_call(
        functools.partial(kernel, sizes=sizes),
        out_shape=jax.ShapeDtypeStruct((nt, bs, bs), f32),
        in_specs=[
            pl.BlockSpec(memory_space=pltpu.HBM),
            pl.BlockSpec(memory_space=pltpu.HBM),
            pl.BlockSpec(memory_space=pltpu.HBM),
        ],
        out_specs=pl.BlockSpec(memory_space=pltpu.VMEM),
        scratch_shapes=scratch,
        compiler_params=pltpu.CompilerParams(
            collective_id=0, has_side_effects=True, vmem_limit_bytes=50 * 2**20
        ),
        cost_estimate=pl.CostEstimate(flops=3 * slots * 2 * bs**3, bytes_accessed=3 * 2**20, transcendentals=0),
    )(*(pltpu.with_memory_space_constraint(x, pltpu.HBM) for x in (pairs, left_own, right_own)))
    return tiles[None, None]


def solution(mesh):
    placed = (
        P("row", "col", "layer", None, None, None),
        P("row", "col", "layer", None, None, None),
        P("row", "col", "layer", None, None, None),
    )
    return jax.shard_map(
        shards,
        mesh=mesh,
        in_specs=placed,
        out_specs=P("row", "col", "layer", None, None),
        check_vma=False,
    )
```

```python
import functools

import jax
import jax.numpy as jnp
from jax import lax
from jax.experimental import pallas as pl
from jax.experimental.pallas import tpu as pltpu
from jax.sharding import PartitionSpec as P

PARTS = ((64, 64), (64, 32, 32), (32, 32, 16, 16, 16, 16))
PIECES = (32, 32, 16, 16, 16, 16)
UNROLL = {128: 68, 64: 68, 48: 68, 32: 68, 16: 68}
DIRECT = ("11", "12", "20", "21", "22", "23", "24", "25")
SCHEDULE = (
    "o0", "c00", "o1", "q", "s00", "c01", "f0", "s01", "o2", "o3", "p", "c10", "s10", "f1", "c20", "s20",
    "f2", "o4", "f3", "o5", "r10", "c11", "s11", "c21", "k20", "s21", "c22", "f4", "s22", "k10", "c23", "f5",
    "k11", "s23", "c12", "k21", "s12", "c24", "k22", "s24", "k23", "c25", "s25", "r00", "k12", "r01", "k24", "k25",
    "k00", "k01", "z21", "z12", "z24", "z20", "z23", "z11", "z22", "z10", "z25",
)


def sort_lists(pairs, chunk_lanes, zero_block, block_count):
    a_row, b_row, c_row = pairs
    slots = c_row.shape[1]
    iota = lambda shape, dim: lax.broadcasted_iota(jnp.int32, shape, dim)
    square = (slots, slots)
    c_across = jnp.broadcast_to(c_row, square)
    c_down = jnp.transpose(c_across)
    earlier = iota(square, 0) < iota(square, 1)
    rank = jnp.sum(jnp.where((c_down == c_across) & earlier, 1, 0), axis=0, keepdims=True)
    group = iota((block_count, slots), 0)
    c_short = jnp.broadcast_to(c_row, (block_count, slots))
    counts = jnp.sum(jnp.where(c_short == group, 1, 0), axis=1, keepdims=True)
    halves = jnp.broadcast_to((counts + 1) >> 1, (block_count, slots))
    before = jnp.sum(jnp.where(group < c_short, halves, 0), axis=0, keepdims=True)
    place = jnp.where(c_row < block_count, 2 * before + rank, 1023)
    first = jnp.where(rank == 0, 1, 0)
    word = place + (a_row << 10) + (b_row << 15) + (c_row << 22) + (first << 28)
    down = jnp.transpose(jnp.broadcast_to(word, square))
    if chunk_lanes != slots:
        down = down[:, :chunk_lanes]
    place = down & 1023
    entry = (((down >> 10) & 31) + 1) + (((down >> 15) & 127) << 8) + (((down >> 28) & 1) << 16)
    c_down = (down >> 22) & 63
    lane = iota((slots, chunk_lanes), 1)
    one = jnp.sum(jnp.where(place == 2 * lane, entry, 0), axis=0, keepdims=True)
    two = jnp.sum(jnp.where(place == 2 * lane + 1, entry, 0), axis=0, keepdims=True)
    last = jnp.max(jnp.where((c_down == lane) & (place < 1023), (place >> 1) + 1, 0), axis=0, keepdims=True)
    rows = []
    for picked in (one, two):
        a = picked & 255
        rows.append(jnp.where(a == 0, zero_block, a - 1))
    for picked in (one, two):
        rows.append((picked >> 8) & 255)
    rows.append(1 - ((one >> 16) & 1))
    rows.append(last)
    return rows


def kernel(pairs_hbm, a_hbm, b_hbm, out_ref, *scratch, sizes):
    n_row, n_col, n_layer, ta, bs, nc, chunks, lanes, parts, pieces, unroll = sizes
    steps = len(parts)
    starts = lambda heights: [sum(heights[:m]) for m in range(len(heights))]
    offsets = [starts(heights) for heights in parts]
    piece_offsets = starts(pieces)
    scratch = list(scratch)

    def take(count):
        taken = scratch[:count]
        del scratch[:count]
        return taken

    def take_parts():
        return [take(len(heights)) for heights in parts]

    a_bufs = take_parts()
    b_buf, pairs_ref = take(2)
    heights_used = sorted({rows for heights in parts for rows in heights})
    products = dict(zip(heights_used, take(len(heights_used))))
    plan_out = take(steps)
    plan_in = take(steps - 1)
    plan_s = take(steps)
    partial, inbox, total, shift = (take_parts() for _ in range(4))
    local_sem, send_sem, recv_sem = take(3)

    r, q, l = lax.axis_index("row"), lax.axis_index("col"), lax.axis_index("layer")

    def at(dr=0, dq=0, dl=0):
        return {
            "row": lax.rem(r + dr + n_row, n_row),
            "col": lax.rem(q + dq + n_col, n_col),
            "layer": lax.rem(l + dl + n_layer, n_layer),
        }

    started = []
    send_slots, recv_slots = {}, {}

    def send_slot(key):
        return send_sem.at[send_slots.setdefault(key, len(send_slots))]

    def recv_slot(key):
        return recv_sem.at[recv_slots.setdefault(key, len(recv_slots))]

    def send(src, dst, target, send_key, recv_key):
        copy = pltpu.make_async_remote_copy(
            src_ref=src,
            dst_ref=dst,
            send_sem=send_slot(send_key),
            recv_sem=recv_slot(recv_key),
            device_id=target,
            device_id_type=pl.DeviceIdType.MESH,
        )
        copy.start()
        return copy

    def wait_bytes(ref, sem):
        pltpu.make_async_copy(ref, ref, sem).wait()

    def local(src, dst):
        copy = pltpu.make_async_copy(src, dst, local_sem.at[len(started)])
        copy.start()
        started.append(copy)
        return copy

    arrived = set()

    def arrive(copy):
        if id(copy) not in arrived:
            arrived.add(id(copy))
            copy.wait_recv()

    nt = nc // n_layer
    half = nt // 2

    barrier = pltpu.get_barrier_semaphore()
    partners = [at(0, 2), at(0, -2), at(-1, 1), at(1, -1), at(0, 1), at(0, -1)]
    partners += [at(0, 0, 1), at(0, 0, -1), at(0, 0, 2)]
    for partner in partners:
        pl.semaphore_signal(barrier, inc=1, device_id=partner, device_id_type=pl.DeviceIdType.MESH)
    own_pairs = local(pairs_hbm, pairs_ref)
    own_a = [
        local(a_hbm.at[:, pl.ds(offset, rows), :], buf.at[pl.ds(0, ta)])
        for offset, rows, buf in zip(offsets[0], parts[0], a_bufs[0])
    ]
    own_b = local(b_hbm, b_buf)

    pl.semaphore_wait(barrier, len(partners))

    next_a = at(1, -1)
    hop1, hop2 = {}, {}

    waited = set()

    def once(copy):
        if id(copy) not in waited:
            waited.add(id(copy))
            copy.wait()

    def members(s, m):
        low, high = offsets[s][m], offsets[s][m] + parts[s][m]
        return [i for i, offset in enumerate(piece_offsets) if low <= offset < high]

    def piece_of(s, i):
        for m in range(len(parts[s])):
            if i in members(s, m):
                return a_bufs[s][m].at[pl.ds(0, ta), pl.ds(piece_offsets[i] - offsets[s][m], pieces[i])]

    def begin(i):
        for m, offset in enumerate(offsets[0]):
            if offset <= piece_offsets[i] < offset + parts[0][m]:
                once(own_a[m])
        hop1[i] = send(piece_of(0, i), piece_of(1, i), next_a, "a", ("first", i))

    def forward(i):
        arrive(hop1[i])
        hop2[i] = send(piece_of(1, i), piece_of(2, i), next_a, "a", ("second", i))

    order = list(SCHEDULE)
    while order[0][0] == "o":
        begin(int(order.pop(0)[1]))

    plan_copy = {}

    def list_step(s):
        listed = sort_lists([pairs_ref[s, i] for i in range(3)], lanes, ta, nc)
        for i, row in enumerate(listed):
            plan_out[s][pl.ds(i, 1), :] = row
        plan_out[s][pl.ds(6, 2), :] = jnp.zeros((2, lanes), jnp.int32)
        if s == 0:
            plan_copy[s] = local(plan_out[0], plan_s[0])
        else:
            plan_copy[s] = send(plan_out[s], plan_in[s - 1], at(0, -s), ("plan", s), ("plan", s))

    own_pairs.wait()
    list_step(0)

    for bufs in a_bufs:
        for buf in bufs:
            buf[ta] = jnp.zeros(buf.shape[1:], buf.dtype)
    for buf in products.values():
        buf[0] = jnp.zeros(buf.shape[1:], buf.dtype)

    def send_plans():
        for s in range(1, steps):
            list_step(s)

    plan_sends = []

    def plans():
        for i in range(1, steps):
            arrive(plan_copy[i])
            plan_sends.append(plan_copy[i])
            plan_copy[i] = local(plan_in[i - 1], plan_s[i])

    def compute(s, m):
        once(plan_copy[s])
        if s == 0:
            once(own_b)
            once(own_a[m])
        else:
            for i in members(s, m):
                arrive((hop1, hop2)[s - 1][i])
        rows = parts[s][m]
        a_buf, plan, target, running_sums = a_bufs[s][m], plan_s[s], partial[s][m], products[rows]

        def one(k, running):
            left = jnp.concatenate([a_buf[plan[0, k]], a_buf[plan[1, k]]], axis=1)
            right = jnp.concatenate([b_buf[plan[2, k]], b_buf[plan[3, k]]], axis=0)
            product = jnp.dot(left, right, preferred_element_type=jnp.float32)
            running = jnp.where(plan[4, k] > 0, running, 0.0) + product
            running_sums[k + 1] = running
            return running

        lax.fori_loop(0, chunks, one, jnp.zeros((rows, bs), jnp.float32), unroll=unroll[rows])
        for c in range(nc):
            target[c] = running_sums[plan[5, c]]

    right, left, across = at(0, 0, 1), at(0, 0, -1), at(0, 0, 2)
    right_at, left_at, across_at = nt * right["layer"], nt * left["layer"], nt * across["layer"]
    shift_copies = {}

    def is_direct(s, m):
        return f"{s}{m}" in DIRECT

    def spread(s, m):
        source, box = partial[s][m], inbox[s][m]

        def pass_on(start, count, slot, target, kind="all"):
            send(source.at[pl.ds(start, count)], box.at[pl.ds(slot, count)], target, s, (kind, s, m))

        if is_direct(s, m):
            pass_on(across_at, nt, 0, across)
            pass_on(right_at, nt, nt, right)
            pass_on(left_at, nt, 2 * nt, left)
            return
        pass_on(across_at, half, 0, right, "far")
        pass_on(across_at + half, half, half, left, "far")
        pass_on(right_at + half, half, nt + half, right)
        pass_on(left_at, half, 2 * nt, left)

    def relay(s, m):
        source, box = partial[s][m], inbox[s][m]
        wait_bytes(box.at[pl.ds(0, nt)], recv_slot(("far", s, m)))
        for start, slot, place, target in ((right_at, 0, nt, right), (left_at + half, half, 2 * nt + half, left)):
            blocks = pl.ds(start, half)
            source[blocks] = source[blocks] + box[pl.ds(slot, half)]
            send(source.at[blocks], box.at[pl.ds(place, half)], target, s, ("all", s, m))

    def collect(s, m):
        box, sem = inbox[s][m], recv_slot(("all", s, m))
        summed = partial[s][m][pl.ds(nt * l, nt)]
        if is_direct(s, m):
            wait_bytes(box, sem)
            summed = summed + box[pl.ds(0, nt)]
        else:
            wait_bytes(box.at[pl.ds(nt, 2 * nt)], sem)
        summed = summed + box[pl.ds(nt, nt)] + box[pl.ds(2 * nt, nt)]
        if s == 0:
            out_ref[:, pl.ds(offsets[s][m], parts[s][m]), :] = summed
        else:
            total[s][m][...] = summed
            shift_copies[s, m] = send(total[s][m], shift[s][m], at(0, s), s, ("shift", s))

    def finish(s, m):
        if s not in arrived:
            arrived.add(s)
            wait_bytes(b_buf.at[pl.ds(0, 2 * nt)], recv_slot(("shift", s)))
        rows = pl.ds(offsets[s][m], parts[s][m])
        out_ref[:, rows, :] = out_ref[:, rows, :] + shift[s][m][...]

    actions = {
        "o": begin,
        "f": forward,
        "c": compute,
        "s": spread,
        "r": relay,
        "k": collect,
        "z": finish,
        "p": plans,
        "q": send_plans,
    }
    for step in order:
        actions[step[0]](*(int(digit) for digit in step[1:]))
    for s in range(steps):
        blocks = 3 * nt + (nt if s else 0)
        wait_bytes(b_buf.at[pl.ds(0, 2 * blocks)], send_slot(s))
    wait_bytes(b_buf.at[pl.ds(0, 2 * ta)], send_slot("a"))
    for copy in plan_sends:
        copy.wait_send()


def shards(left_panels, right_panels, pair_lists):
    left_own = left_panels[0, 0, 0]
    right_own = right_panels[0, 0, 0]
    pairs = pair_lists[0, 0, 0][:, :, None, :]
    ta, bs, _ = left_own.shape
    tb = right_own.shape[0]
    steps, _, _, slots = pairs.shape
    nc = 16
    n_row, n_col, n_layer = (lax.axis_size(axis) for axis in ("row", "col", "layer"))
    nt = nc // n_layer
    parts = tuple(tuple(rows * bs // 128 for rows in heights) for heights in PARTS)
    pieces = tuple(rows * bs // 128 for rows in PIECES)
    chunks = (slots + nc) // 2
    unroll = {rows * bs // 128: by if chunks % by == 0 else 2 for rows, by in UNROLL.items()}
    f32, i32, bf16 = jnp.float32, jnp.int32, left_own.dtype
    vmem = pltpu.VMEM
    every = [rows for heights in parts for rows in heights]
    scratch = [vmem((ta + 1, rows, bs), bf16) for rows in every]
    scratch += [vmem((tb, bs, bs), bf16), vmem(pairs.shape, i32)]
    scratch += [vmem((chunks + 1, rows, bs), f32) for rows in sorted(set(every))]
    scratch += [vmem((8, slots), i32) for _ in range(2 * steps - 1)]
    scratch += [pltpu.SMEM((8, slots), i32) for _ in range(steps)]
    for blocks in (nc, 3 * nt, nt, nt):
        scratch += [vmem((blocks, rows, bs), f32) for rows in every]
    sends = steps + 1 + steps - 1
    receives = 2 * len(pieces) + 2 * (steps - 1) + 2 * len(every) - len(DIRECT)
    scratch += [pltpu.SemaphoreType.DMA((len(parts[0]) + steps + 2,))]
    scratch += [pltpu.SemaphoreType.DMA((sends,)), pltpu.SemaphoreType.DMA((receives,))]
    sizes = (n_row, n_col, n_layer, ta, bs, nc, chunks, slots, parts, pieces, unroll)
    tiles = pl.pallas_call(
        functools.partial(kernel, sizes=sizes),
        out_shape=jax.ShapeDtypeStruct((nt, bs, bs), f32),
        in_specs=[
            pl.BlockSpec(memory_space=pltpu.HBM),
            pl.BlockSpec(memory_space=pltpu.HBM),
            pl.BlockSpec(memory_space=pltpu.HBM),
        ],
        out_specs=pl.BlockSpec(memory_space=pltpu.VMEM),
        scratch_shapes=scratch,
        compiler_params=pltpu.CompilerParams(
            collective_id=0, has_side_effects=True, vmem_limit_bytes=50 * 2**20
        ),
        cost_estimate=pl.CostEstimate(flops=3 * slots * 2 * bs**3, bytes_accessed=3 * 2**20, transcendentals=0),
    )(*(pltpu.with_memory_space_constraint(x, pltpu.HBM) for x in (pairs, left_own, right_own)))
    return tiles[None, None]


def solution(mesh):
    placed = (
        P("row", "col", "layer", None, None, None),
        P("row", "col", "layer", None, None, None),
        P("row", "col", "layer", None, None, None),
    )
    return jax.shard_map(
        shards,
        mesh=mesh,
        in_specs=placed,
        out_specs=P("row", "col", "layer", None, None),
        check_vma=False,
    )
```
